256 devices in a mesh: segment: 16 (over z_lo, y), seq: 16 (over z_hi, x, core).
Axes of the slice: x: 4, y: 4, z: 8 (z_hi: 2, z_lo: 4; z = z_hi * 4 + z_lo), core: 2. Of those that a mesh axis runs over, the one named last changes fastest.
Arguments:
- queue: bfloat16 [16, 2048, 3072], P('segment', 'seq'), may hold values from -4 to 4
- fresh_noise: bfloat16 [2048, 3072], P('seq'), may hold values from -6 to 6
- w_mod: bfloat16 [16, 3072, 9216], P('segment', None, 'seq'), may hold values from -0.109375 to 0.109375
- w_qkv: bfloat16 [16, 3072, 16, 384], P('segment', None, 'seq'), may hold values from -0.109375 to 0.109375
- w_out: bfloat16 [16, 2048, 3072], P('segment', 'seq'), may hold values from -0.125 to 0.125
- q_gain: float32 [16, 128], P('segment'), may hold values from 1.5 to 7, as said below
- k_gain: float32 [16, 128], P('segment'), may hold values from 1.5 to 7, as said below
- levels: int32 [16], P('segment'), may hold values from 0 to 49
- plan: int32 [50], replicated, may hold values from 0 to 999
- positions: int32 [16], P('segment'), may hold values from 0 to 1023
Outputs:
- queue_next: bfloat16 [16, 2048, 3072], P('segment', 'seq')
- clean_frame: bfloat16 [2048, 3072], P('seq', 'segment')
The draws below stay inside these ranges and needn't reach their ends.
Inputs may be any that keep to these rules, and one draw needn't show every extreme that they name: `q_gain`: query gains are positive. `k_gain`: key gains are positive.
All inputs are finite; a program needn't handle non-finite values.
Results may differ from the reference program's by a relative error of at most 0.035.
Values may be sent and summed in bfloat16 or wider, within the bound.
No kernel may reach another device: no remote copies, remote signals or barrier semaphores. Data moves between devices by JAX's collectives and lax.ppermute only.
A program may use at most 128 MiB of HBM per device.

```python
import jax
import jax.numpy as jnp
from jax import lax

D = 3072
HEAD_DIM = 128
HEAD_DEV = 1
GRID_W = 32
LEVELS = 50
HEADS = 16
TOK_F = 2048
FRAMES = 16
N_SEQ = 16


def gain_values(key, lowest, highest):
    return jnp.exp(jax.random.uniform(key, (FRAMES, HEAD_DIM), jnp.float32, jnp.log(lowest), jnp.log(highest)))


def draw_q_gain(key, part):
    key = jax.random.fold_in(key, 11)
    return gain_values(key, 1.5, 3.0)


def draw_k_gain(key, part):
    key = jax.random.fold_in(key, 23)
    return gain_values(key, 1.5, 3.0)


def touch_ends(values, rng, least, largest):
    spot = [jax.random.randint(jax.random.fold_in(rng, axis), (), 0, length) for axis, length in enumerate(values.shape)]
    widest = values.shape.index(max(values.shape))
    neighbour = spot[:widest] + [(spot[widest] + 1) % values.shape[widest]] + spot[widest + 1:]
    return values.at[tuple(spot)].set(least).at[tuple(neighbour)].set(largest)


def block_scale(own_key, dims, pieces, least, largest):
    loudness = 1.0
    for dim, blocks in pieces:
        steps = jax.random.uniform(jax.random.fold_in(jax.random.fold_in(own_key, 6), dim), (blocks,), jnp.float32, least / len(pieces), largest / len(pieces))
        loudness = loudness * jnp.repeat(jnp.exp(steps), dims[dim] // blocks).reshape((-1,) + (1,) * (len(dims) - 1 - dim))
    return loudness


def centred(rng, extent, scale, reach, split=(), held_as=jnp.bfloat16):
    values = scale * jax.random.normal(rng, extent, jnp.float32)
    if split:
        values = values * block_scale(rng, extent, split, -0.22, 0.18)
    return jnp.clip(values, -reach, reach).astype(held_as)


def setup_inputs(seed: int = 0) -> dict:
    arg_keys = jax.random.split(jax.random.key(seed), 11)
    queue = centred(arg_keys[0], (FRAMES, TOK_F, D), 0.5, 4.0, ((0, 16), (1, 16)))
    fresh_noise = centred(arg_keys[1], (TOK_F, D), 1.0, 6.0, ((0, 16),))
    w_mod = centred(arg_keys[2], (FRAMES, D, 3 * D), D ** -0.5, 0.109375, ((0, 16), (2, 16)))
    w_qkv = centred(arg_keys[3], (FRAMES, D, HEADS, 3 * HEAD_DIM), D ** -0.5, 0.109375, ((0, 16), (2, 16)))
    w_out = centred(arg_keys[4], (FRAMES, HEADS * HEAD_DIM, D), (HEADS * HEAD_DIM) ** -0.5, 0.125, ((0, 16), (1, 16)))
    q_gain = draw_q_gain(jax.random.fold_in(arg_keys[10], 71), 0)
    k_gain = draw_k_gain(jax.random.fold_in(arg_keys[10], 71), 0)
    levels = touch_ends(jax.random.randint(arg_keys[7], (FRAMES,), 0, LEVELS), jax.random.fold_in(arg_keys[7], 1), 0, LEVELS - 1).astype(jnp.int32)
    plan = touch_ends(jax.random.randint(arg_keys[8], (LEVELS,), 0, 1000), jax.random.fold_in(arg_keys[8], 1), 0, 999).astype(jnp.int32)
    positions = touch_ends(jax.random.randint(arg_keys[9], (FRAMES,), 0, 1024), jax.random.fold_in(arg_keys[9], 1), 0, 1023).astype(jnp.int32)
    return dict(queue=queue, fresh_noise=fresh_noise, w_mod=w_mod, w_qkv=w_qkv, w_out=w_out, q_gain=q_gain, k_gain=k_gain, levels=levels, plan=plan, positions=positions)


EPSILON = 1e-06
ROPE_BASE = 256.0

def time_embedding(step_values, width):
    half_width = width // 2
    counter = jnp.arange(half_width, dtype=jnp.float32)
    frequency = jnp.exp(-jnp.log(10000.0) * counter / half_width)
    angles = step_values.astype(jnp.float32)[:, None] * frequency[None, :]
    return jnp.concatenate([jnp.cos(angles), jnp.sin(angles)], axis=-1)

def rope_angles(frame_position, row_count, head_dim, grid_width):
    time_dim = head_dim // 8
    space_dim = (head_dim - time_dim) // 2
    tokens_at = jnp.arange(row_count, dtype=jnp.int32)
    grid_row = (tokens_at // grid_width).astype(jnp.float32)
    grid_col = (tokens_at % grid_width).astype(jnp.float32)
    moment = jnp.zeros((row_count,), jnp.float32) + frame_position.astype(jnp.float32)
    sections = []
    for coords, section in ((moment, time_dim), (grid_row, space_dim), (grid_col, space_dim)):
        half_size = section // 2
        frequency = ROPE_BASE ** (-2.0 * jnp.arange(half_size, dtype=jnp.float32) / section)
        angles = coords[:, None] * frequency[None, :]
        sections.append(jnp.concatenate([angles, angles], axis=-1))
    return jnp.concatenate(sections, axis=-1)

def rotate_half(values, head_dim):
    time_dim = head_dim // 8
    space_dim = (head_dim - time_dim) // 2
    pieces_out = []
    position = 0
    for section in (time_dim, space_dim, space_dim):
        half_size = section // 2
        leading = values[..., position:position + half_size]
        second = values[..., position + half_size:position + section]
        pieces_out.append(jnp.concatenate([-second, leading], axis=-1))
        position += section
    return jnp.concatenate(pieces_out, axis=-1)

def apply_rope(values, angles, head_dim):
    return values * jnp.cos(angles) + rotate_half(values, head_dim) * jnp.sin(angles)

def rms_gain(values, gains):
    mean_square = lax.optimization_barrier(jnp.mean(values * values, axis=-1, keepdims=True))
    return values * lax.rsqrt(mean_square + EPSILON) * gains

def layer_norm(values):
    centre = lax.optimization_barrier(jnp.mean(values, axis=-1, keepdims=True))
    spread = lax.optimization_barrier(jnp.mean(jnp.square(values - centre), axis=-1, keepdims=True))
    return (values - centre) * lax.rsqrt(spread + EPSILON)

def attend(query_rows, key_rows, value_rows, usable, head_dim):
    scores = jnp.dot(query_rows, key_rows.T, preferred_element_type=jnp.float32) * head_dim ** (-0.5)
    scores = jnp.where(usable[None, :], scores, -jnp.inf)
    row_max = lax.optimization_barrier(jnp.max(scores, axis=-1, keepdims=True))
    raised = jnp.exp(scores - row_max)
    weights = (raised / lax.optimization_barrier(jnp.sum(raised, axis=-1, keepdims=True))).astype(jnp.bfloat16)
    return jnp.dot(weights, value_rows, preferred_element_type=jnp.float32).astype(jnp.bfloat16)

def reference(queue, fresh_noise, w_mod, w_qkv, w_out, q_gain, k_gain, levels, plan, positions):
    picked = levels[:, None] == jnp.arange(LEVELS, dtype=jnp.int32)[None, :]
    step_values = lax.optimization_barrier(jnp.sum(jnp.where(picked, plan[None, :], 0), axis=1)).astype(jnp.int32)
    embedding = jax.nn.silu(time_embedding(step_values, D)).astype(jnp.bfloat16)

    def modulate_one(inputs):
        emb_row, weight = inputs
        return jnp.dot(emb_row[None, :], weight, preferred_element_type=jnp.float32)[0]
    modulation = lax.map(modulate_one, (embedding, w_mod))

    def project_one(inputs):
        frame, mod_row, weight, gain_q, gain_k, frame_position = inputs
        shift_row = mod_row[:D]
        scale_row = mod_row[D:2 * D]
        normed = layer_norm(frame.astype(jnp.float32))
        modulated = (normed * (1.0 + scale_row) + shift_row).astype(jnp.bfloat16)
        projected_qkv = jnp.dot(modulated, weight.reshape(D, HEADS * 3 * HEAD_DIM), preferred_element_type=jnp.float32)
        projected_qkv = projected_qkv.reshape(TOK_F, HEADS, 3 * HEAD_DIM)
        angles = rope_angles(frame_position, TOK_F, HEAD_DIM, GRID_W)[:, None, :]
        queries = apply_rope(rms_gain(projected_qkv[..., :HEAD_DIM], gain_q), angles, HEAD_DIM).astype(jnp.bfloat16)
        key_rows = apply_rope(rms_gain(projected_qkv[..., HEAD_DIM:2 * HEAD_DIM], gain_k), angles, HEAD_DIM).astype(jnp.bfloat16)
        value_rows = projected_qkv[..., 2 * HEAD_DIM:].astype(jnp.bfloat16)
        return (queries, key_rows, value_rows)
    query_all, key_all, value_all = lax.map(project_one, (queue, modulation, w_qkv, q_gain, k_gain, positions))

    def block_one(frame_at):
        before = jnp.maximum(frame_at - 1, 0)
        after = jnp.minimum(frame_at + 1, FRAMES - 1)
        near_keys = jnp.concatenate([key_all[before], key_all[frame_at], key_all[after]], axis=0)
        near_values = jnp.concatenate([value_all[before], value_all[frame_at], value_all[after]], axis=0)
        filled = jnp.ones((TOK_F,), dtype=bool)
        usable = jnp.concatenate([filled & (frame_at > 0), filled, filled & (frame_at < FRAMES - 1)])
        own_queries = query_all[frame_at]

        def head_one(head_at):
            return attend(own_queries[:, head_at], near_keys[:, head_at], near_values[:, head_at], usable, HEAD_DIM)
        attended = lax.map(head_one, jnp.arange(HEADS, dtype=jnp.int32))
        attended = jnp.transpose(attended, (1, 0, 2)).reshape(TOK_F, N_SEQ, HEAD_DEV * HEAD_DIM)
        grouped_rows = w_out[frame_at].reshape(N_SEQ, HEAD_DEV * HEAD_DIM, D)

        def add_group(running, inputs):
            rows_in, weight = inputs
            partial_value = jnp.dot(rows_in, weight, preferred_element_type=jnp.float32).astype(jnp.bfloat16)
            partial_value = lax.optimization_barrier(partial_value)
            return (running + partial_value.astype(jnp.float32), None)
        projected, _ = lax.scan(add_group, jnp.zeros((TOK_F, D), jnp.float32), (jnp.transpose(attended, (1, 0, 2)), grouped_rows))
        gate_row = modulation[frame_at, 2 * D:]
        return (queue[frame_at].astype(jnp.float32) + gate_row * projected).astype(jnp.bfloat16)
    finished = lax.map(block_one, jnp.arange(FRAMES, dtype=jnp.int32))
    queue_next = jnp.concatenate([fresh_noise[None], finished[:-1]], axis=0)
    return (queue_next, finished[FRAMES - 1])
```

```python
import functools
import math

import jax
import jax.numpy as jnp
import numpy as np
from jax import lax
from jax.experimental import pallas as pl
from jax.experimental.pallas import tpu as pltpu
from jax.sharding import PartitionSpec as P

GRID_W = 32
EPSILON = 1e-06
ROPE_BASE = 256.0
HEAD = 128
NEG = -1e30
XN, CN, ZN = 4, 2, 2
VMEM = pl.BlockSpec(memory_space=pltpu.VMEM)
SMEM = pl.BlockSpec(memory_space=pltpu.SMEM)
LIMIT = 48 << 20


def seq_id(z, x, c):
    return (z % ZN) * XN * CN + (x % XN) * CN + (c % CN)


ALL = [(z, x, c) for z in range(ZN) for x in range(XN) for c in range(CN)]
X_UP = [(seq_id(z, x, c), seq_id(z, x + 1, c)) for z, x, c in ALL]
X_DOWN = [(seq_id(z, x, c), seq_id(z, x - 1, c)) for z, x, c in ALL]
X_FAR = [(seq_id(z, x, c), seq_id(z, x + 2, c)) for z, x, c in ALL]
Z_SWAP = [(seq_id(z, x, c), seq_id(z + 1, x, c)) for z, x, c in ALL]
C_SWAP = [(seq_id(z, x, c), seq_id(z, x, c + 1)) for z, x, c in ALL]


def on_seq(value, pairs):
    return lax.ppermute(value, "seq", pairs)


def lane_order():
    time_dim = HEAD // 8
    space_dim = (HEAD - time_dim) // 2
    first, second, start = [], [], 0
    for section in (time_dim, space_dim, space_dim):
        half = section // 2
        first += list(range(start, start + half))
        second += list(range(start + half, start + section))
        start += section
    return np.array(first + second)


ORDER = lane_order()


def order_matrix():
    one = np.zeros((3 * HEAD, 3 * HEAD), np.float32)
    for part in range(2):
        one[part * HEAD + ORDER, part * HEAD + np.arange(HEAD)] = 1.0
    one[2 * HEAD + np.arange(HEAD), 2 * HEAD + np.arange(HEAD)] = 1.0
    return one


def time_embedding(step_values, width):
    half_width = width // 2
    counter = jnp.arange(half_width, dtype=jnp.float32)
    frequency = jnp.exp(-jnp.log(10000.0) * counter / half_width)
    angles = step_values.astype(jnp.float32)[:, None] * frequency[None, :]
    return jnp.concatenate([jnp.cos(angles), jnp.sin(angles)], axis=-1)


def rope_tables(position, seq_places, tok_dev):
    time_dim = HEAD // 8
    space_dim = (HEAD - time_dim) // 2
    token = jnp.arange(tok_dev, dtype=jnp.int32)
    whole = jnp.concatenate([place * tok_dev + token for place in seq_places])
    grid_row = (whole // GRID_W).astype(jnp.float32)
    grid_col = (whole % GRID_W).astype(jnp.float32)
    moment = jnp.zeros_like(grid_row) + position.astype(jnp.float32)
    sections = []
    for coords, section in ((moment, time_dim), (grid_row, space_dim), (grid_col, space_dim)):
        half_size = section // 2
        frequency = ROPE_BASE ** (-2.0 * jnp.arange(half_size, dtype=jnp.float32) / section)
        sections.append(coords[:, None] * frequency[None, :])
    angles = jnp.concatenate(sections * 2, axis=-1)
    sign = jnp.where(jnp.arange(HEAD) < HEAD // 2, -1.0, 1.0)
    return jnp.cos(angles), jnp.sin(angles) * sign


def norm_kernel(x_ref, o_ref):
    x = x_ref[...].astype(jnp.float32)
    centre = jnp.mean(x, axis=-1, keepdims=True)
    x = x - centre
    spread = jnp.mean(x * x, axis=-1, keepdims=True)
    o_ref[...] = (x * lax.rsqrt(spread + EPSILON)).astype(jnp.bfloat16)


def norm_rows(x):
    rows, width = x.shape
    block = 32
    return pl.pallas_call(
        norm_kernel,
        grid=(rows // block,),
        in_specs=[pl.BlockSpec((block, width), lambda i: (i, 0))],
        out_specs=pl.BlockSpec((block, width), lambda i: (i, 0)),
        out_shape=jax.ShapeDtypeStruct(x.shape, jnp.bfloat16),
        cost_estimate=pl.CostEstimate(flops=8 * x.size, bytes_accessed=4 * x.size, transcendentals=0),
        name="norm_rows",
    )(x)


def qkv_kernel(count, scale_ref, shift_ref, cos_ref, sin_ref, gq_ref, gk_ref, w_mine, w_other, *refs):
    x_refs = refs[:count]
    q_mine, kv_mine, q_other, kv_other, acc = refs[count:]
    step = pl.program_id(0)
    x = jnp.concatenate([r[...] for r in x_refs], axis=0).astype(jnp.float32)
    x = (x * scale_ref[...] + shift_ref[...]).astype(jnp.bfloat16)
    w = jnp.concatenate([w_mine[...], w_other[...]], axis=1)
    part = jnp.dot(x, w, preferred_element_type=jnp.float32)

    @pl.when(step == 0)
    def _():
        acc[...] = part

    @pl.when(step > 0)
    def _():
        acc[...] += part

    @pl.when(step == pl.num_programs(0) - 1)
    def _():
        cos, sin = cos_ref[...], sin_ref[...]

        def turned(y, gain):
            y = y * lax.rsqrt(jnp.mean(y * y, axis=-1, keepdims=True) + EPSILON) * gain
            return (y * cos + pltpu.roll(y, HEAD // 2, 1) * sin).astype(jnp.bfloat16)

        for at, q_ref, kv_ref in ((0, q_mine, kv_mine), (3 * HEAD, q_other, kv_other)):
            q_ref[...] = turned(acc[:, at : at + HEAD], gq_ref[...])
            kv_ref[:, :HEAD] = turned(acc[:, at + HEAD : at + 2 * HEAD], gk_ref[...])
            kv_ref[:, HEAD:] = acc[:, at + 2 * HEAD : at + 3 * HEAD].astype(jnp.bfloat16)


def qkv(blocks, scale, shift, cos, sin, gq, gk, w_mine, w_other):
    width = w_mine.shape[0]
    rows = sum(b.shape[0] for b in blocks)
    depth = 512
    row_spec = pl.BlockSpec((1, depth), lambda k: (0, k))
    whole = lambda a: pl.BlockSpec(a.shape, lambda k: (0, 0))
    w_spec = pl.BlockSpec((depth, 3 * HEAD), lambda k: (k, 0))
    out = [jax.ShapeDtypeStruct((rows, n), jnp.bfloat16) for n in (HEAD, 2 * HEAD, HEAD, 2 * HEAD)]
    return pl.pallas_call(
        functools.partial(qkv_kernel, len(blocks)),
        grid=(width // depth,),
        in_specs=[row_spec, row_spec, whole(cos), whole(sin), whole(gq), whole(gk), w_spec, w_spec]
        + [pl.BlockSpec((b.shape[0], depth), lambda k: (0, k)) for b in blocks],
        out_specs=[pl.BlockSpec(o.shape, lambda k: (0, 0)) for o in out],
        out_shape=out,
        scratch_shapes=[pltpu.VMEM((rows, 6 * HEAD), jnp.float32)],
        compiler_params=pltpu.CompilerParams(vmem_limit_bytes=LIMIT),
        cost_estimate=pl.CostEstimate(
            flops=2 * rows * width * 6 * HEAD, bytes_accessed=2 * width * (6 * HEAD + rows), transcendentals=0
        ),
        name="qkv",
    )(scale, shift, cos, sin, gq, gk, w_mine, w_other, *blocks)


def attend_kernel(flag_ref, *refs):
    q_refs, kv_refs, o_ref = refs[:4], refs[4:16], refs[16]
    qb = q_refs[0].shape[0]
    for at in range(4):
        q = q_refs[at][...]
        acc = m = None
        for group in range(3):
            flag = None if group == 0 else flag_ref[group - 1] > 0
            scores = [
                lax.dot_general(
                    q,
                    kv_refs[4 * group + j][:, :HEAD],
                    (((1,), (1,)), ((), ())),
                    preferred_element_type=jnp.float32,
                )
                for j in range(4)
            ]
            top = functools.reduce(jnp.maximum, [jnp.max(s, axis=1, keepdims=True) for s in scores])
            if flag is not None:
                top = jnp.where(flag, top, NEG)
            after = top if m is None else jnp.maximum(m, top)
            less = after if flag is None else jnp.where(flag, after, -NEG)
            total = None
            for j in range(4):
                p = jnp.exp2(scores[j] - less).astype(jnp.bfloat16)
                v = kv_refs[4 * group + j][:, HEAD:]
                v = jnp.concatenate([v, jnp.ones_like(v)], axis=1)
                d = jnp.dot(p, v, preferred_element_type=jnp.float32)
                total = d if total is None else total + d
            acc = total if acc is None else acc * jnp.exp2(m - after) + total
            m = after
        o_ref[at * qb : (at + 1) * qb, :] = (acc[:, :HEAD] / acc[:, HEAD:]).astype(jnp.bfloat16)


def attend(flags, queries, key_values):
    rows = sum(q.shape[0] for q in queries)
    keys = sum(k.shape[0] for k in key_values)
    return pl.pallas_call(
        attend_kernel,
        in_specs=[SMEM] + [VMEM] * (len(queries) + len(key_values)),
        out_specs=VMEM,
        out_shape=jax.ShapeDtypeStruct((rows, HEAD), jnp.bfloat16),
        compiler_params=pltpu.CompilerParams(vmem_limit_bytes=LIMIT),
        cost_estimate=pl.CostEstimate(
            flops=4 * rows * keys * HEAD * 2, bytes_accessed=512 * (rows + keys), transcendentals=rows * keys
        ),
        name="attend",
    )(flags, *queries, *key_values)


def out_kernel(count, *refs):
    a_refs = refs[:4]
    w_refs = refs[4 : 4 + count]
    mine, other = refs[4 + count :]
    a = jnp.concatenate([r[...] for r in a_refs], axis=1)
    w = jnp.concatenate([r[...] for r in w_refs], axis=0)
    part = jnp.dot(a, w, preferred_element_type=jnp.float32)
    rows = mine.shape[0]
    mine[...] = part[:rows]
    other[...] = part[rows:].astype(jnp.bfloat16)


def out_project(a_parts, w_parts):
    rows = a_parts[0].shape[0] // 2
    width = w_parts[0].shape[1]
    depth = sum(w.shape[0] for w in w_parts)
    step = 512
    return pl.pallas_call(
        functools.partial(out_kernel, len(w_parts)),
        grid=(width // step,),
        in_specs=[pl.BlockSpec(a.shape, lambda n: (0, 0)) for a in a_parts]
        + [pl.BlockSpec((w.shape[0], step), lambda n: (0, n)) for w in w_parts],
        out_specs=[pl.BlockSpec((rows, step), lambda n: (0, n))] * 2,
        out_shape=[
            jax.ShapeDtypeStruct((rows, width), jnp.float32),
            jax.ShapeDtypeStruct((rows, width), jnp.bfloat16),
        ],
        compiler_params=pltpu.CompilerParams(vmem_limit_bytes=LIMIT),
        cost_estimate=pl.CostEstimate(
            flops=4 * rows * width * depth, bytes_accessed=2 * width * (depth + 3 * rows), transcendentals=0
        ),
        name="out_project",
    )(*a_parts, *w_parts)


def ring_gather(own):
    half = own.shape[0] // 2
    below = on_seq(own, X_UP)
    above = on_seq(own, X_DOWN)
    far_top = on_seq(below[:half], X_UP)
    far_low = on_seq(above[half:], X_DOWN)
    return [own, below, above, far_top, far_low]


def gathered_modulation(part, x, c, z):
    up, down, far = on_seq(part, X_UP), on_seq(part, X_DOWN), on_seq(part, X_FAR)
    ring = jnp.concatenate([part, down, far, up], axis=0)
    ring = lax.dynamic_slice_in_dim(jnp.concatenate([ring, ring], axis=0), (XN - x) % XN, XN, axis=0)
    got = on_seq(ring, C_SWAP)
    pair = jnp.where(c == 0, jnp.stack([ring, got], axis=1), jnp.stack([got, ring], axis=1))
    got = on_seq(pair, Z_SWAP)
    both = jnp.where(z == 0, jnp.stack([pair, got]), jnp.stack([got, pair]))
    return both.reshape(1, -1)


def shards(queue, fresh_noise, w_mod, w_qkv, w_out, q_gain, k_gain, levels, plan, positions):
    segments = lax.axis_size("segment")
    segment_at = lax.axis_index("segment")
    seq_at = lax.axis_index("seq")
    z, x, c = seq_at // (XN * CN), (seq_at // CN) % XN, seq_at % CN
    tok_dev, width = queue.shape[1], queue.shape[2]

    picked = levels[:, None] == jnp.arange(plan.shape[0], dtype=jnp.int32)[None, :]
    step_values = jnp.sum(jnp.where(picked, plan[None, :], 0), axis=1)
    embedding = jax.nn.silu(time_embedding(step_values, width)).astype(jnp.bfloat16)
    mod_part = jnp.dot(embedding, w_mod[0], preferred_element_type=jnp.float32)
    modulation = gathered_modulation(mod_part, x, c, z)
    shift_row = modulation[:, :width]
    scale_row = 1.0 + modulation[:, width : 2 * width]
    gate_row = modulation[:, 2 * width :]

    order = jnp.asarray(order_matrix(), jnp.bfloat16)
    w_raw = w_qkv[0].reshape(width, 3 * HEAD)
    w_got = on_seq(w_raw, C_SWAP)
    w_mine = jnp.dot(w_raw, order, preferred_element_type=jnp.float32).astype(jnp.bfloat16)
    w_other = jnp.dot(w_got, order, preferred_element_type=jnp.float32).astype(jnp.bfloat16)
    gq = q_gain[:, ORDER] * (HEAD**-0.5 * math.log2(math.e))
    gk = k_gain[:, ORDER]

    normed = norm_rows(queue[0])
    z_normed = on_seq(normed, Z_SWAP)
    halves = []
    for zz, block in ((z, normed), (1 - z, z_normed)):
        blocks = ring_gather(block)
        places = [zz * XN * CN + ((x + r) % XN) * CN + c for r in (0, XN - 1, 1, 2)]
        cos, sin = rope_tables(positions[0], places, tok_dev)
        q_mine, kv_mine, q_other, kv_other = qkv(
            blocks, scale_row, shift_row, cos, sin, gq, gk, w_mine, w_other
        )
        halves += [(q_mine, kv_mine), (on_seq(q_other, C_SWAP), on_seq(kv_other, C_SWAP))]
    up = [(i, i + 1) for i in range(segments - 1)]
    down = [(i + 1, i) for i in range(segments - 1)]
    own_kv = [kv for _, kv in halves]
    before = [lax.ppermute(kv, "segment", up) for kv in own_kv]
    after = [lax.ppermute(kv, "segment", down) for kv in own_kv]
    flags = jnp.stack([segment_at > 0, segment_at < segments - 1]).astype(jnp.int32)
    attended = attend(flags, [q for q, _ in halves], own_kv + before + after)

    w_blocks = [ring_gather(w_out[0]), ring_gather(on_seq(w_out[0], Z_SWAP))]
    w_parts = []
    for at in range(4):
        for side in w_blocks:
            w_parts += side[at : at + 1] if at < 3 else side[3:5]
    near = attended[: 8 * tok_dev]
    far = on_seq(attended[8 * tok_dev :], Z_SWAP)
    heads = jnp.stack([near.reshape(2, 4, tok_dev, HEAD), far.reshape(2, 4, tok_dev, HEAD)], axis=3)
    heads = heads.reshape(2, 4, tok_dev, 2 * HEAD)
    side = lambda r: heads[:, r].reshape(2 * tok_dev, 2 * HEAD)
    a_parts = [side(0), on_seq(side(2), X_UP), on_seq(side(1), X_DOWN), on_seq(side(3), X_FAR)]
    mine, other = out_project(a_parts, w_parts)
    projected = mine + on_seq(other, C_SWAP).astype(jnp.float32)
    finished = (queue[0].astype(jnp.float32) + gate_row * projected).astype(jnp.bfloat16)

    arrived = lax.ppermute(finished, "segment", up)
    queue_next = jnp.where(segment_at == 0, fresh_noise, arrived)[None]

    side_n = 4
    columns = width // segments
    last = segments - 1
    piece = lambda at: finished[:, at * columns : (at + 1) * columns]
    spread = jnp.where(
        segment_at == last,
        jnp.concatenate([piece(side_n * i + side_n - 1) for i in range(side_n)], axis=1),
        jnp.zeros((), jnp.bfloat16),
    )
    for place in range(side_n - 1):
        sent = jnp.concatenate([piece(side_n * i + place) for i in range(side_n)], axis=1)
        spread += lax.ppermute(sent, "segment", [(last, last - (side_n - 1) + place)])
    clean = jnp.where(segment_at >= segments - side_n, spread[:, (side_n - 1) * columns :], jnp.zeros((), jnp.bfloat16))
    for row in range(side_n - 1):
        clean += lax.ppermute(
            spread[:, row * columns : (row + 1) * columns],
            "segment",
            [(segments - side_n + place, row * side_n + place) for place in range(side_n)],
        )
    return (queue_next, clean)


def solution(mesh):
    placed = (
        P("segment", "seq", None),
        P("seq", None),
        P("segment", None, "seq"),
        P("segment", None, "seq", None),
        P("segment", "seq", None),
        P("segment", None),
        P("segment", None),
        P("segment"),
        P(),
        P("segment"),
    )
    return jax.shard_map(
        shards,
        mesh=mesh,
        in_specs=placed,
        out_specs=(P("segment", "seq", None), P("seq", "segment")),
        check_vma=False,
    )
```

```python
import functools
import math

import jax
import jax.numpy as jnp
import numpy as np
from jax import lax
from jax.experimental import pallas as pl
from jax.experimental.pallas import tpu as pltpu
from jax.sharding import PartitionSpec as P

GRID_W = 32
EPSILON = 1e-06
ROPE_BASE = 256.0
HEAD = 128
NEG = -1e30
XN, CN, ZN = 4, 2, 2
VMEM = pl.BlockSpec(memory_space=pltpu.VMEM)
SMEM = pl.BlockSpec(memory_space=pltpu.SMEM)
LIMIT = 32 << 20


def seq_id(z, x, c):
    return (z % ZN) * XN * CN + (x % XN) * CN + (c % CN)


ALL = [(z, x, c) for z in range(ZN) for x in range(XN) for c in range(CN)]
X_UP = [(seq_id(z, x, c), seq_id(z, x + 1, c)) for z, x, c in ALL]
X_DOWN = [(seq_id(z, x, c), seq_id(z, x - 1, c)) for z, x, c in ALL]
X_FAR = [(seq_id(z, x, c), seq_id(z, x + 2, c)) for z, x, c in ALL]
X_PAIR = [(seq_id(z, x, c), seq_id(z, x ^ 1, c)) for z, x, c in ALL]
Z_SWAP = [(seq_id(z, x, c), seq_id(z + 1, x, c)) for z, x, c in ALL]
C_SWAP = [(seq_id(z, x, c), seq_id(z, x, c + 1)) for z, x, c in ALL]


def on_seq(value, pairs):
    return lax.ppermute(value, "seq", pairs)


def tie(*values):
    return lax.optimization_barrier(values)


def lane_order():
    time_dim = HEAD // 8
    space_dim = (HEAD - time_dim) // 2
    first, second, start = [], [], 0
    for section in (time_dim, space_dim, space_dim):
        half = section // 2
        first += list(range(start, start + half))
        second += list(range(start + half, start + section))
        start += section
    return np.array(first + second)


ORDER = lane_order()


def order_matrix():
    one = np.zeros((3 * HEAD, 3 * HEAD), np.float32)
    for part in range(2):
        one[part * HEAD + ORDER, part * HEAD + np.arange(HEAD)] = 1.0
    one[2 * HEAD + np.arange(HEAD), 2 * HEAD + np.arange(HEAD)] = 1.0
    return one


def time_embedding(step_values, width):
    half_width = width // 2
    counter = jnp.arange(half_width, dtype=jnp.float32)
    frequency = jnp.exp(-jnp.log(10000.0) * counter / half_width)
    angles = step_values.astype(jnp.float32)[:, None] * frequency[None, :]
    return jnp.concatenate([jnp.cos(angles), jnp.sin(angles)], axis=-1)


def rope_frequencies():
    time_dim = HEAD // 8
    space_dim = (HEAD - time_dim) // 2
    lanes = np.zeros((3, HEAD), np.float32)
    start = 0
    for at, section in enumerate((time_dim, space_dim, space_dim)):
        half = section // 2
        power = np.float32(ROPE_BASE) ** (np.float32(-2.0) * np.arange(half, dtype=np.float32) / np.float32(section))
        lanes[at, start : start + half] = power
        lanes[at, HEAD // 2 + start : HEAD // 2 + start + half] = power
        start += half
    return lanes


def rope_tables(position, places, tok_dev):
    lanes = jnp.asarray(rope_frequencies())
    sign = jnp.where(jnp.arange(HEAD) < HEAD // 2, -1.0, 1.0)
    rows = tok_dev // GRID_W
    grid_row = (jnp.stack(places)[:, None] * rows + jnp.arange(rows, dtype=jnp.int32)).astype(jnp.float32)
    grid_col = jnp.arange(GRID_W, dtype=jnp.int32).astype(jnp.float32)
    by_row = position.astype(jnp.float32) * lanes[0] + grid_row[..., None] * lanes[1]
    by_col = grid_col[:, None] * lanes[2]
    column = lanes[2] > 0
    tables = []
    for turn, factor in ((jnp.cos, 1.0), (jnp.sin, sign)):
        table = jnp.where(column, (turn(by_col) * factor)[None, None], (turn(by_row) * factor)[:, :, None])
        tables.append(table.reshape(-1, HEAD))
    return tuple(tables)


def norm_kernel(x_ref, o_ref):
    x = x_ref[...].astype(jnp.float32)
    centre = jnp.mean(x, axis=-1, keepdims=True)
    x = x - centre
    spread = jnp.mean(x * x, axis=-1, keepdims=True)
    o_ref[...] = (x * lax.rsqrt(spread + EPSILON)).astype(jnp.bfloat16)


def norm_rows(x):
    rows, width = x.shape
    block = 64
    return pl.pallas_call(
        norm_kernel,
        grid=(rows // block,),
        in_specs=[pl.BlockSpec((block, width), lambda i: (i, 0))],
        out_specs=pl.BlockSpec((block, width), lambda i: (i, 0)),
        out_shape=jax.ShapeDtypeStruct(x.shape, jnp.bfloat16),
        cost_estimate=pl.CostEstimate(flops=1, bytes_accessed=1, transcendentals=0),
        name="norm_rows",
    )(x)


def qkv_kernel(count, scale_ref, shift_ref, cos_ref, sin_ref, gq_ref, gk_ref, w_mine, w_other, *refs):
    x_refs = refs[:count]
    q_mine, kv_mine, all_other, acc = refs[count:]
    step = pl.program_id(0)
    x = jnp.concatenate([r[...] for r in x_refs], axis=0).astype(jnp.float32)
    x = (x * scale_ref[...] + shift_ref[...]).astype(jnp.bfloat16)
    w = jnp.concatenate([w_mine[...], w_other[...]], axis=1)
    part = jnp.dot(x, w, preferred_element_type=jnp.float32)

    @pl.when(step == 0)
    def _():
        acc[...] = part

    @pl.when(step > 0)
    def _():
        acc[...] += part

    @pl.when(step == pl.num_programs(0) - 1)
    def _():
        cos, sin = cos_ref[...], sin_ref[...]

        def turned(y, gain):
            y = y * lax.rsqrt(jnp.mean(y * y, axis=-1, keepdims=True) + EPSILON) * gain
            return (y * cos + pltpu.roll(y, HEAD // 2, 1) * sin).astype(jnp.bfloat16)

        q_mine[...] = turned(acc[:, :HEAD], gq_ref[...])
        kv_mine[:, :HEAD] = turned(acc[:, HEAD : 2 * HEAD], gk_ref[...])
        kv_mine[:, HEAD:] = acc[:, 2 * HEAD : 3 * HEAD].astype(jnp.bfloat16)
        all_other[:, :HEAD] = turned(acc[:, 3 * HEAD : 4 * HEAD], gq_ref[...])
        all_other[:, HEAD : 2 * HEAD] = turned(acc[:, 4 * HEAD : 5 * HEAD], gk_ref[...])
        all_other[:, 2 * HEAD :] = acc[:, 5 * HEAD :].astype(jnp.bfloat16)


def qkv(limit, blocks, scale, shift, cos, sin, gq, gk, w_mine, w_other):
    width = w_mine.shape[0]
    rows = sum(b.shape[0] for b in blocks)
    depth = 1536
    row_spec = pl.BlockSpec((1, depth), lambda k: (0, k))
    whole = lambda a: pl.BlockSpec(a.shape, lambda k: (0, 0))
    w_spec = pl.BlockSpec((depth, 3 * HEAD), lambda k: (k, 0))
    out = [jax.ShapeDtypeStruct((rows, n), jnp.bfloat16) for n in (HEAD, 2 * HEAD, 3 * HEAD)]
    return pl.pallas_call(
        functools.partial(qkv_kernel, len(blocks)),
        grid=(width // depth,),
        in_specs=[row_spec, row_spec, whole(cos), whole(sin), whole(gq), whole(gk), w_spec, w_spec]
        + [pl.BlockSpec((b.shape[0], depth), lambda k: (0, k)) for b in blocks],
        out_specs=[pl.BlockSpec(o.shape, lambda k: (0, 0)) for o in out],
        out_shape=out,
        scratch_shapes=[pltpu.VMEM((rows, 6 * HEAD), jnp.float32)],
        compiler_params=pltpu.CompilerParams(vmem_limit_bytes=limit),
        cost_estimate=pl.CostEstimate(flops=1, bytes_accessed=1, transcendentals=0),
        name="qkv",
    )(scale, shift, cos, sin, gq, gk, w_mine, w_other, *blocks)


def attend_kernel(flag_ref, *refs):
    q_in, kv_in, o_refs = refs[:4], refs[4:10], refs[10:12]
    q_a, q_b, kv_all, sems = refs[12:]
    kv_refs = [kv_all.at[i] for i in range(6)]
    copies = [pltpu.make_async_copy(q_in[i], (q_a, q_b)[i % 2].at[i // 2], sems.at[6 + i]) for i in range(4)]
    copies += [pltpu.make_async_copy(kv_in[i], kv_refs[i], sems.at[i]) for i in range(6)]
    for copy in copies:
        copy.start()
    for copy in copies[:4]:
        copy.wait()
    blocks = q_a.shape[1] // HEAD
    chunk = 512
    per = kv_all.shape[1] // chunk
    state = [(None, None)] * 4
    for group in range(3):
        flag = None if group == 0 else flag_ref[group - 1] > 0
        parts = [(kv_refs[2 * group + i], j * chunk) for i in range(2) for j in range(per)]
        for copy in copies[4 + 2 * group : 6 + 2 * group]:
            copy.wait()
        for at, q_ref in enumerate((q_a.at[0], q_b.at[0], q_a.at[1], q_b.at[1])):
            q = q_ref[:, :HEAD]
            acc, m = state[at]
            scores = [
                lax.dot_general(
                    q,
                    ref[row : row + chunk, :HEAD],
                    (((1,), (1,)), ((), ())),
                    preferred_element_type=jnp.float32,
                )
                for ref, row in parts
            ]
            top = functools.reduce(jnp.maximum, [jnp.max(s, axis=1, keepdims=True) for s in scores])
            if flag is not None:
                top = jnp.where(flag, top, NEG)
            later = top if m is None else jnp.maximum(m, top)
            less = later if flag is None else jnp.where(flag, later, -NEG)
            total = None
            for score, (ref, row) in zip(scores, parts):
                p = jnp.exp2(score - less).astype(jnp.bfloat16)
                v = ref[row : row + chunk, HEAD:]
                v = jnp.concatenate([v, jnp.ones_like(v)], axis=1)
                d = jnp.dot(p, v, preferred_element_type=jnp.float32)
                total = d if total is None else total + d
            acc = total if acc is None else acc * jnp.exp2(m - later) + total
            state[at] = (acc, later)
    for at, (acc, _) in enumerate(state):
        o = (acc[:, :HEAD] / acc[:, HEAD:]).astype(jnp.bfloat16)
        for block in range(blocks):
            row = (2 * block + at % 2) * HEAD
            o_refs[at // 2][row : row + HEAD, :] = o[block * HEAD : (block + 1) * HEAD]


def attend(flags, queries, key_values):
    rows = 2 * queries[0].shape[0]
    return pl.pallas_call(
        attend_kernel,
        in_specs=[SMEM] + [pl.BlockSpec(memory_space=pl.ANY)] * (4 + len(key_values)),
        out_specs=[VMEM] * 2,
        out_shape=[jax.ShapeDtypeStruct((rows, HEAD), jnp.bfloat16)] * 2,
        scratch_shapes=[
            pltpu.VMEM((2, *queries[0].shape), jnp.bfloat16),
            pltpu.VMEM((2, *queries[1].shape), jnp.bfloat16),
            pltpu.VMEM((len(key_values), *key_values[0].shape), jnp.bfloat16),
            pltpu.SemaphoreType.DMA((4 + len(key_values),)),
        ],
        compiler_params=pltpu.CompilerParams(vmem_limit_bytes=60 << 20),
        cost_estimate=pl.CostEstimate(flops=1, bytes_accessed=1, transcendentals=0),
        name="attend",
    )(flags, *queries, *key_values)


def pair_kernel(near_ref, far_ref, *outs):
    rows = outs[0].shape[0]
    for at, out in enumerate(outs):
        out[:, :HEAD] = near_ref[at * rows : (at + 1) * rows, :]
        out[:, HEAD:] = far_ref[at * rows : (at + 1) * rows, :]


def pair_heads(near, far):
    rows = near.shape[0] // XN
    return pl.pallas_call(
        pair_kernel,
        in_specs=[VMEM] * 2,
        out_specs=[VMEM] * XN,
        out_shape=[jax.ShapeDtypeStruct((rows, 2 * HEAD), jnp.bfloat16)] * XN,
        cost_estimate=pl.CostEstimate(flops=1, bytes_accessed=1, transcendentals=0),
        name="pair_heads",
    )(near, far)


def out_kernel(count, *refs):
    a_refs = refs[:4]
    w_refs = refs[4 : 4 + count]
    mine, other = refs[4 + count :]
    a = jnp.concatenate([r[...] for r in a_refs], axis=1)
    w = jnp.concatenate([r[...] for r in w_refs], axis=0)
    part = jnp.dot(a, w, preferred_element_type=jnp.float32)
    rows = mine.shape[0]
    mine[...] = part[:rows]
    other[...] = part[rows:].astype(jnp.bfloat16)


def out_project(a_parts, w_parts):
    rows = a_parts[0].shape[0] // 2
    width = w_parts[0].shape[1]
    depth = sum(w.shape[0] for w in w_parts)
    step = 512
    return pl.pallas_call(
        functools.partial(out_kernel, len(w_parts)),
        grid=(width // step,),
        in_specs=[pl.BlockSpec(a.shape, lambda n: (0, 0)) for a in a_parts]
        + [pl.BlockSpec((w.shape[0], step), lambda n: (0, n)) for w in w_parts],
        out_specs=[pl.BlockSpec((rows, step), lambda n: (0, n))] * 2,
        out_shape=[
            jax.ShapeDtypeStruct((rows, width), jnp.float32),
            jax.ShapeDtypeStruct((rows, width), jnp.bfloat16),
        ],
        compiler_params=pltpu.CompilerParams(vmem_limit_bytes=60 << 20),
        cost_estimate=pl.CostEstimate(flops=1, bytes_accessed=1, transcendentals=0),
        name="out_project",
    )(*a_parts, *w_parts)


def gather_step(part, pairs, bit):
    got = on_seq(part, pairs)
    return jnp.concatenate([jnp.where(bit == 0, part, got), jnp.where(bit == 0, got, part)], axis=0)


def finish_kernel(side_n, queue_ref, gate_ref, mine_ref, got_ref, sent_ref, *pieces):
    width = queue_ref.shape[1]
    columns = width // (side_n * side_n)
    projected = mine_ref[...] + got_ref[...].astype(jnp.float32)
    finished = (queue_ref[...].astype(jnp.float32) + gate_ref[...] * projected).astype(jnp.bfloat16)
    for place, piece in enumerate(pieces):
        for row in range(side_n):
            at = (row * side_n + place) * columns
            piece[:, row * columns : (row + 1) * columns] = finished[:, at : at + columns]
    sent_ref[...] = finished


def finish(side_n, queue, gate, mine, got):
    rows, width = queue.shape
    step = 32
    spec = lambda n: pl.BlockSpec((step, n), lambda i: (i, 0))
    out = [jax.ShapeDtypeStruct((rows, width), jnp.bfloat16)]
    out += [jax.ShapeDtypeStruct((rows, width // side_n), jnp.bfloat16)] * side_n
    return pl.pallas_call(
        functools.partial(finish_kernel, side_n),
        grid=(rows // step,),
        in_specs=[spec(width), pl.BlockSpec((1, width), lambda i: (0, 0)), spec(width), spec(width)],
        out_specs=[spec(o.shape[1]) for o in out],
        out_shape=out,
        compiler_params=pltpu.CompilerParams(vmem_limit_bytes=60 << 20),
        cost_estimate=pl.CostEstimate(flops=1, bytes_accessed=1, transcendentals=0),
        name="finish",
    )(queue, gate, mine, got)


def shards(queue, fresh_noise, w_mod, w_qkv, w_out, q_gain, k_gain, levels, plan, positions):
    segments = lax.axis_size("segment")
    segment_at = lax.axis_index("segment")
    seq_at = lax.axis_index("seq")
    z, x, c = seq_at // (XN * CN), (seq_at // CN) % XN, seq_at % CN
    tok_dev, width = queue.shape[1], queue.shape[2]
    up = [(i, (i + 1) % segments) for i in range(segments)]
    down = [((i + 1) % segments, i) for i in range(segments)]

    half = tok_dev // 2
    one_hot = order_matrix()
    order = jnp.asarray(one_hot, jnp.bfloat16)

    def ordered(w):
        return jnp.dot(w, order, preferred_element_type=jnp.float32).astype(jnp.bfloat16)

    def table(zz, position):
        places = [zz * XN * CN + ((x + r) % XN) * CN + c for r in (0, XN - 1, 1, 2)]
        return rope_tables(position, places, tok_dev)

    w_raw = w_qkv[0].reshape(width, 3 * HEAD)
    w_out_own = w_out[0]
    w_got = on_seq(w_raw, C_SWAP)
    normed = norm_rows(queue[0])
    z_normed, below, above = on_seq(normed, Z_SWAP), on_seq(normed, X_UP), on_seq(normed, X_DOWN)

    levels, normed = tie(levels, normed)
    picked = levels[:, None] == jnp.arange(plan.shape[0], dtype=jnp.int32)[None, :]
    step_values = jnp.sum(jnp.where(picked, plan[None, :], 0), axis=1)
    embedding = jax.nn.silu(time_embedding(step_values, width)).astype(jnp.bfloat16)
    mod = jnp.dot(embedding, w_mod[0], preferred_element_type=jnp.float32)
    mod, w_raw = tie(mod, w_raw)
    w_mine = ordered(w_raw)
    mod = gather_step(mod, C_SWAP, c)
    mod, w_mine, below, above, positions = tie(mod, w_mine, below, above, positions)
    top, low = below[:half], above[half:]
    mod = gather_step(mod, X_PAIR, x % 2)
    mod, top, low, positions = tie(mod, top, low, positions)
    far_top, far_low = on_seq(top, X_UP), on_seq(low, X_DOWN)
    near_table = table(z, positions[0])
    mod = gather_step(mod, X_FAR, x // 2)
    mod, w_got, positions, *near_table = tie(mod, w_got, positions, *near_table)
    w_other = ordered(w_got)
    mod = gather_step(mod, Z_SWAP, z)
    gains = jnp.sum(jnp.concatenate([q_gain, k_gain])[:, :, None] * jnp.asarray(one_hot[None, :HEAD, :HEAD]), axis=1)
    gq = gains[:1] * (HEAD**-0.5 * math.log2(math.e))
    gk = gains[1:]
    z_normed, far_top, far_low, w_out_own, positions, gq, gk = tie(
        z_normed, far_top, far_low, w_out_own, positions, gq, gk
    )
    z_below, z_above = on_seq(z_normed, X_UP), on_seq(z_normed, X_DOWN)
    w_far = on_seq(w_out_own, Z_SWAP)
    far_table = table(1 - z, positions[0])
    modulation = mod.reshape(1, -1)
    shift_row = modulation[:, :width]
    scale_row = 1.0 + modulation[:, width : 2 * width]
    gate_row = modulation[:, 2 * width :]

    def half_frame(limit, blocks, tables):
        return qkv(limit, blocks, scale_row, shift_row, *tables, gq, gk, w_mine, w_other)

    def with_partner(q_mine, kv_mine, other):
        got = on_seq(other, C_SWAP)
        return (q_mine, got), jnp.concatenate([kv_mine, got[:, HEAD:]], axis=0)

    def halo(kv):
        return lax.ppermute(kv, "segment", up), lax.ppermute(kv, "segment", down)

    near_half = half_frame(60 << 20, (normed, below, above, far_top, far_low), near_table)
    z_below, z_above, *near_half = tie(z_below, z_above, *near_half)
    top, low = z_below[:half], z_above[half:]
    top, low, w_out_own, *near_half = tie(top, low, w_out_own, *near_half)
    w_below, w_above = on_seq(w_out_own, X_UP), on_seq(w_out_own, X_DOWN)
    z_far_top, z_far_low = on_seq(top, X_UP), on_seq(low, X_DOWN)
    q_near, kv_near = with_partner(*near_half)
    halo_near = halo(kv_near)
    z_normed, z_far_top, kv_near, w_far = tie(z_normed, z_far_top, kv_near, w_far)
    far_half = half_frame(LIMIT, (z_normed, z_below, z_above, z_far_top, z_far_low), far_table)
    q_far, kv_far = with_partner(*far_half)
    kv_far, *halo_near = tie(kv_far, *halo_near)
    halo_far = halo(kv_far)
    kv_far, w_below, w_above = tie(kv_far, w_below, w_above)
    top, low = w_below[:half], w_above[half:]
    top, low, w_far, *halo_far = tie(top, low, w_far, *halo_far)
    near_w = [w_out_own, w_below, w_above, on_seq(top, X_UP), on_seq(low, X_DOWN)]

    flags = jnp.stack([segment_at > 0, segment_at < segments - 1]).astype(jnp.int32)
    w_below, w_above = on_seq(w_far, X_UP), on_seq(w_far, X_DOWN)
    key_values = (kv_near, kv_far, halo_near[0], halo_far[0], halo_near[1], halo_far[1])
    near, theirs = attend(flags, (*q_near, *q_far), key_values)
    far = on_seq(theirs, Z_SWAP)
    near, w_below, w_above = tie(near, w_below, w_above)
    top, low = w_below[:half], w_above[half:]
    near, top, low = tie(near, top, low)
    far_w = [w_far, w_below, w_above, on_seq(top, X_UP), on_seq(low, X_DOWN)]
    sides = pair_heads(near, far)
    a_parts = [sides[0], on_seq(sides[2], X_UP), on_seq(sides[1], X_DOWN), on_seq(sides[3], X_FAR)]
    w_parts = []
    for at in range(4):
        for block in (near_w, far_w):
            w_parts += block[at : at + 1] if at < 3 else block[3:5]
    mine, other = out_project(a_parts, w_parts)
    side_n = 4
    last = segments - 1
    finished, *pieces = finish(side_n, queue[0], gate_row, mine, on_seq(other, C_SWAP))
    arrived = lax.ppermute(finished, "segment", up[:-1])
    queue_next = jnp.where(segment_at == 0, fresh_noise, arrived)[None]

    columns = width // segments
    spread = jnp.where(segment_at == last, pieces[-1], jnp.zeros((), jnp.bfloat16))
    for place in range(side_n - 1):
        spread += lax.ppermute(pieces[place], "segment", [(last, last - (side_n - 1) + place)])
    clean = jnp.where(segment_at >= segments - side_n, spread[:, (side_n - 1) * columns :], jnp.zeros((), jnp.bfloat16))
    for row in range(side_n - 1):
        clean += lax.ppermute(
            spread[:, row * columns : (row + 1) * columns],
            "segment",
            [(segments - side_n + place, row * side_n + place) for place in range(side_n)],
        )
    return (queue_next, clean)


def solution(mesh):
    placed = (
        P("segment", "seq", None),
        P("seq", None),
        P("segment", None, "seq"),
        P("segment", None, "seq", None),
        P("segment", "seq", None),
        P("segment", None),
        P("segment", None),
        P("segment"),
        P(),
        P("segment"),
    )
    return jax.shard_map(
        shards,
        mesh=mesh,
        in_specs=placed,
        out_specs=(P("segment", "seq", None), P("seq", "segment")),
        check_vma=False,
    )
```

```python
import functools
import math

import jax
import jax.numpy as jnp
import numpy as np
from jax import lax
from jax.experimental import pallas as pl
from jax.experimental.pallas import tpu as pltpu
from jax.sharding import PartitionSpec as P

GRID_W = 32
EPSILON = 1e-06
ROPE_BASE = 256.0
HEAD = 128
NEG = -1e30
XN, CN, ZN = 4, 2, 2
VMEM = pl.BlockSpec(memory_space=pltpu.VMEM)
SMEM = pl.BlockSpec(memory_space=pltpu.SMEM)
LIMIT = 32 << 20


def seq_id(z, x, c):
    return (z % ZN) * XN * CN + (x % XN) * CN + (c % CN)


ALL = [(z, x, c) for z in range(ZN) for x in range(XN) for c in range(CN)]
X_UP = [(seq_id(z, x, c), seq_id(z, x + 1, c)) for z, x, c in ALL]
X_DOWN = [(seq_id(z, x, c), seq_id(z, x - 1, c)) for z, x, c in ALL]
X_FAR = [(seq_id(z, x, c), seq_id(z, x + 2, c)) for z, x, c in ALL]
X_PAIR = [(seq_id(z, x, c), seq_id(z, x ^ 1, c)) for z, x, c in ALL]
Z_SWAP = [(seq_id(z, x, c), seq_id(z + 1, x, c)) for z, x, c in ALL]
C_SWAP = [(seq_id(z, x, c), seq_id(z, x, c + 1)) for z, x, c in ALL]


def on_seq(value, pairs):
    return lax.ppermute(value, "seq", pairs)


def tie(*values):
    return lax.optimization_barrier(values)


def lane_order():
    time_dim = HEAD // 8
    space_dim = (HEAD - time_dim) // 2
    first, second, start = [], [], 0
    for section in (time_dim, space_dim, space_dim):
        half = section // 2
        first += list(range(start, start + half))
        second += list(range(start + half, start + section))
        start += section
    return np.array(first + second)


ORDER = lane_order()


def order_matrix():
    one = np.zeros((3 * HEAD, 3 * HEAD), np.float32)
    for part in range(2):
        one[part * HEAD + ORDER, part * HEAD + np.arange(HEAD)] = 1.0
    one[2 * HEAD + np.arange(HEAD), 2 * HEAD + np.arange(HEAD)] = 1.0
    return one


def time_embedding(step_values, width):
    half_width = width // 2
    counter = jnp.arange(half_width, dtype=jnp.float32)
    frequency = jnp.exp(-jnp.log(10000.0) * counter / half_width)
    angles = step_values.astype(jnp.float32)[:, None] * frequency[None, :]
    return jnp.concatenate([jnp.cos(angles), jnp.sin(angles)], axis=-1)


def rope_frequencies():
    time_dim = HEAD // 8
    space_dim = (HEAD - time_dim) // 2
    lanes = np.zeros((3, HEAD), np.float32)
    start = 0
    for at, section in enumerate((time_dim, space_dim, space_dim)):
        half = section // 2
        power = np.float32(ROPE_BASE) ** (np.float32(-2.0) * np.arange(half, dtype=np.float32) / np.float32(section))
        lanes[at, start : start + half] = power
        lanes[at, HEAD // 2 + start : HEAD // 2 + start + half] = power
        start += half
    return lanes


def rope_tables(position, places, tok_dev):
    lanes = jnp.asarray(rope_frequencies())
    sign = jnp.where(jnp.arange(HEAD) < HEAD // 2, -1.0, 1.0)
    rows = tok_dev // GRID_W
    grid_row = (jnp.stack(places)[:, None] * rows + jnp.arange(rows, dtype=jnp.int32)).astype(jnp.float32)
    grid_col = jnp.arange(GRID_W, dtype=jnp.int32).astype(jnp.float32)
    by_row = position.astype(jnp.float32) * lanes[0] + grid_row[..., None] * lanes[1]
    by_col = grid_col[:, None] * lanes[2]
    column = lanes[2] > 0
    tables = []
    for turn, factor in ((jnp.cos, 1.0), (jnp.sin, sign)):
        table = jnp.where(column, (turn(by_col) * factor)[None, None], (turn(by_row) * factor)[:, :, None])
        tables.append(table.reshape(-1, HEAD))
    return tuple(tables)


def norm_kernel(x_ref, o_ref):
    x = x_ref[...].astype(jnp.float32)
    centre = jnp.mean(x, axis=-1, keepdims=True)
    x = x - centre
    spread = jnp.mean(x * x, axis=-1, keepdims=True)
    o_ref[...] = (x * lax.rsqrt(spread + EPSILON)).astype(jnp.bfloat16)


def norm_rows(x):
    rows, width = x.shape
    block = 64
    return pl.pallas_call(
        norm_kernel,
        grid=(rows // block,),
        in_specs=[pl.BlockSpec((block, width), lambda i: (i, 0))],
        out_specs=pl.BlockSpec((block, width), lambda i: (i, 0)),
        out_shape=jax.ShapeDtypeStruct(x.shape, jnp.bfloat16),
        cost_estimate=pl.CostEstimate(flops=1, bytes_accessed=1, transcendentals=0),
        name="norm_rows",
    )(x)


def qkv_kernel(count, scale_ref, shift_ref, cos_ref, sin_ref, gq_ref, gk_ref, w_mine, w_other, *refs):
    x_refs = refs[:count]
    q_mine, kv_mine, all_other, acc = refs[count:]
    step = pl.program_id(0)
    x = jnp.concatenate([r[...] for r in x_refs], axis=0).astype(jnp.float32)
    x = (x * scale_ref[...] + shift_ref[...]).astype(jnp.bfloat16)
    w = jnp.concatenate([w_mine[...], w_other[...]], axis=1)
    part = jnp.dot(x, w, preferred_element_type=jnp.float32)

    @pl.when(step == 0)
    def _():
        acc[...] = part

    @pl.when(step > 0)
    def _():
        acc[...] += part

    @pl.when(step == pl.num_programs(0) - 1)
    def _():
        cos, sin = cos_ref[...], sin_ref[...]

        def turned(y, gain):
            y = y * lax.rsqrt(jnp.mean(y * y, axis=-1, keepdims=True) + EPSILON) * gain
            return (y * cos + pltpu.roll(y, HEAD // 2, 1) * sin).astype(jnp.bfloat16)

        q_mine[...] = turned(acc[:, :HEAD], gq_ref[...])
        kv_mine[:, :HEAD] = turned(acc[:, HEAD : 2 * HEAD], gk_ref[...])
        kv_mine[:, HEAD:] = acc[:, 2 * HEAD : 3 * HEAD].astype(jnp.bfloat16)
        all_other[:, :HEAD] = turned(acc[:, 3 * HEAD : 4 * HEAD], gq_ref[...])
        all_other[:, HEAD : 2 * HEAD] = turned(acc[:, 4 * HEAD : 5 * HEAD], gk_ref[...])
        all_other[:, 2 * HEAD :] = acc[:, 5 * HEAD :].astype(jnp.bfloat16)


def qkv(limit, blocks, scale, shift, cos, sin, gq, gk, w_mine, w_other):
    width = w_mine.shape[0]
    rows = sum(b.shape[0] for b in blocks)
    depth = 1536
    row_spec = pl.BlockSpec((1, depth), lambda k: (0, k))
    whole = lambda a: pl.BlockSpec(a.shape, lambda k: (0, 0))
    w_spec = pl.BlockSpec((depth, 3 * HEAD), lambda k: (k, 0))
    out = [jax.ShapeDtypeStruct((rows, n), jnp.bfloat16) for n in (HEAD, 2 * HEAD, 3 * HEAD)]
    return pl.pallas_call(
        functools.partial(qkv_kernel, len(blocks)),
        grid=(width // depth,),
        in_specs=[row_spec, row_spec, whole(cos), whole(sin), whole(gq), whole(gk), w_spec, w_spec]
        + [pl.BlockSpec((b.shape[0], depth), lambda k: (0, k)) for b in blocks],
        out_specs=[pl.BlockSpec(o.shape, lambda k: (0, 0)) for o in out],
        out_shape=out,
        scratch_shapes=[pltpu.VMEM((rows, 6 * HEAD), jnp.float32)],
        compiler_params=pltpu.CompilerParams(vmem_limit_bytes=limit),
        cost_estimate=pl.CostEstimate(flops=1, bytes_accessed=1, transcendentals=0),
        name="qkv",
    )(scale, shift, cos, sin, gq, gk, w_mine, w_other, *blocks)


def attend_kernel(groups, count, last, flag_ref, *refs):
    taken = 4 + count + (2 if last else 0)
    q_in, kv_in, state_in = refs[:4], refs[4 : 4 + count], refs[4 + count : taken]
    outs = refs[taken : taken + 2]
    q_a, q_b, kv_all, sems, *state = refs[taken + 2 :]
    copies = [pltpu.make_async_copy(q_in[i], (q_a, q_b)[i % 2].at[i // 2], sems.at[i]) for i in range(4)]
    copies += [pltpu.make_async_copy(kv_in[i], kv_all.at[i], sems.at[4 + i]) for i in range(count)]
    copies += [pltpu.make_async_copy(old, new, sems.at[4 + count + i]) for i, (old, new) in enumerate(zip(state_in, state))]
    for copy in copies:
        copy.start()
    for copy in copies[:4]:
        copy.wait()
    rows = q_a.shape[1]
    chunk = 512
    per = kv_all.shape[1] // chunk
    carried = [(None, None)] * 4
    for flag, arrays in groups:
        exists = None if flag is None else flag_ref[flag] > 0
        parts = [(kv_all.at[i], j * chunk) for i in arrays for j in range(per)]
        for i in arrays:
            copies[4 + i].wait()
        for at, q_ref in enumerate((q_a.at[0], q_b.at[0], q_a.at[1], q_b.at[1])):
            q = q_ref[:, :HEAD]
            acc, m = carried[at]
            scores = [
                lax.dot_general(
                    q,
                    ref[row : row + chunk, :HEAD],
                    (((1,), (1,)), ((), ())),
                    preferred_element_type=jnp.float32,
                )
                for ref, row in parts
            ]
            top = functools.reduce(jnp.maximum, [jnp.max(s, axis=1, keepdims=True) for s in scores])
            if exists is not None:
                top = jnp.where(exists, top, NEG)
            later = top if m is None else jnp.maximum(m, top)
            less = later if exists is None else jnp.where(exists, later, -NEG)
            total = None
            for score, (ref, row) in zip(scores, parts):
                p = jnp.exp2(score - less).astype(jnp.bfloat16)
                v = ref[row : row + chunk, HEAD:]
                v = jnp.concatenate([v, jnp.ones_like(v)], axis=1)
                d = jnp.dot(p, v, preferred_element_type=jnp.float32)
                total = d if total is None else total + d
            acc = total if acc is None else acc * jnp.exp2(m - later) + total
            carried[at] = (acc, later)
    if not last:
        for at, (acc, m) in enumerate(carried):
            place = slice(at * rows, (at + 1) * rows)
            outs[0][place, :] = acc[:, :HEAD] / acc[:, HEAD:]
            outs[1][place, :] = m + jnp.log2(acc[:, HEAD:])
        return
    for copy in copies[4 + count :]:
        copy.wait()
    for at, (acc, m) in enumerate(carried):
        place = slice(at * rows, (at + 1) * rows)
        old_m = state[1][place, :]
        later = jnp.maximum(m, old_m)
        old, new = jnp.exp2(old_m - later), jnp.exp2(m - later)
        o = (state[0][place, :] * old + acc[:, :HEAD] * new) / (old + acc[:, HEAD:] * new)
        for block in range(rows // HEAD):
            row = (2 * block + at % 2) * HEAD
            outs[at // 2][row : row + HEAD, :] = o[block * HEAD : (block + 1) * HEAD].astype(jnp.bfloat16)


def attend(flags, queries, key_values, groups, state=()):
    last = len(state) > 0
    rows = 4 * queries[0].shape[0]
    count = len(key_values)
    if last:
        out = [jax.ShapeDtypeStruct((rows // 2, HEAD), jnp.bfloat16)] * 2
    else:
        out = [jax.ShapeDtypeStruct((rows, HEAD), jnp.float32)] * 2
    return pl.pallas_call(
        functools.partial(attend_kernel, groups, count, last),
        in_specs=[SMEM] + [pl.BlockSpec(memory_space=pl.ANY)] * (4 + count + len(state)),
        out_specs=[VMEM] * 2,
        out_shape=out,
        scratch_shapes=[
            pltpu.VMEM((2, *queries[0].shape), jnp.bfloat16),
            pltpu.VMEM((2, *queries[1].shape), jnp.bfloat16),
            pltpu.VMEM((count, *key_values[0].shape), jnp.bfloat16),
            pltpu.SemaphoreType.DMA((4 + count + len(state),)),
        ]
        + [pltpu.VMEM(x.shape, x.dtype) for x in state],
        compiler_params=pltpu.CompilerParams(vmem_limit_bytes=60 << 20),
        cost_estimate=pl.CostEstimate(flops=1, bytes_accessed=1, transcendentals=0),
        name="attend_rest" if last else "attend_first",
    )(flags, *queries, *key_values, *state)


def pair_kernel(near_ref, far_ref, *outs):
    rows = outs[0].shape[0]
    for at, out in enumerate(outs):
        out[:, :HEAD] = near_ref[at * rows : (at + 1) * rows, :]
        out[:, HEAD:] = far_ref[at * rows : (at + 1) * rows, :]


def pair_heads(near, far):
    rows = near.shape[0] // XN
    return pl.pallas_call(
        pair_kernel,
        in_specs=[VMEM] * 2,
        out_specs=[VMEM] * XN,
        out_shape=[jax.ShapeDtypeStruct((rows, 2 * HEAD), jnp.bfloat16)] * XN,
        cost_estimate=pl.CostEstimate(flops=1, bytes_accessed=1, transcendentals=0),
        name="pair_heads",
    )(near, far)


def out_kernel(count, *refs):
    a_refs = refs[:4]
    w_refs = refs[4 : 4 + count]
    mine, other = refs[4 + count :]
    a = jnp.concatenate([r[...] for r in a_refs], axis=1)
    w = jnp.concatenate([r[...] for r in w_refs], axis=0)
    part = jnp.dot(a, w, preferred_element_type=jnp.float32)
    rows = mine.shape[0]
    mine[...] = part[:rows]
    other[...] = part[rows:].astype(jnp.bfloat16)


def out_project(a_parts, w_parts):
    rows = a_parts[0].shape[0] // 2
    width = w_parts[0].shape[1]
    depth = sum(w.shape[0] for w in w_parts)
    step = 512
    return pl.pallas_call(
        functools.partial(out_kernel, len(w_parts)),
        grid=(width // step,),
        in_specs=[pl.BlockSpec(a.shape, lambda n: (0, 0)) for a in a_parts]
        + [pl.BlockSpec((w.shape[0], step), lambda n: (0, n)) for w in w_parts],
        out_specs=[pl.BlockSpec((rows, step), lambda n: (0, n))] * 2,
        out_shape=[
            jax.ShapeDtypeStruct((rows, width), jnp.float32),
            jax.ShapeDtypeStruct((rows, width), jnp.bfloat16),
        ],
        compiler_params=pltpu.CompilerParams(vmem_limit_bytes=60 << 20),
        cost_estimate=pl.CostEstimate(flops=1, bytes_accessed=1, transcendentals=0),
        name="out_project",
    )(*a_parts, *w_parts)


def gather_step(part, pairs, bit):
    got = on_seq(part, pairs)
    return jnp.concatenate([jnp.where(bit == 0, part, got), jnp.where(bit == 0, got, part)], axis=0)


def finish_kernel(side_n, queue_ref, gate_ref, mine_ref, got_ref, sent_ref, *pieces):
    width = queue_ref.shape[1]
    columns = width // (side_n * side_n)
    projected = mine_ref[...] + got_ref[...].astype(jnp.float32)
    finished = (queue_ref[...].astype(jnp.float32) + gate_ref[...] * projected).astype(jnp.bfloat16)
    for place, piece in enumerate(pieces):
        for row in range(side_n):
            at = (row * side_n + place) * columns
            piece[:, row * columns : (row + 1) * columns] = finished[:, at : at + columns]
    sent_ref[...] = finished


def finish(side_n, queue, gate, mine, got):
    rows, width = queue.shape
    step = 32
    spec = lambda n: pl.BlockSpec((step, n), lambda i: (i, 0))
    out = [jax.ShapeDtypeStruct((rows, width), jnp.bfloat16)]
    out += [jax.ShapeDtypeStruct((rows, width // side_n), jnp.bfloat16)] * side_n
    return pl.pallas_call(
        functools.partial(finish_kernel, side_n),
        grid=(rows // step,),
        in_specs=[spec(width), pl.BlockSpec((1, width), lambda i: (0, 0)), spec(width), spec(width)],
        out_specs=[spec(o.shape[1]) for o in out],
        out_shape=out,
        compiler_params=pltpu.CompilerParams(vmem_limit_bytes=60 << 20),
        cost_estimate=pl.CostEstimate(flops=1, bytes_accessed=1, transcendentals=0),
        name="finish",
    )(queue, gate, mine, got)


def shards(queue, fresh_noise, w_mod, w_qkv, w_out, q_gain, k_gain, levels, plan, positions):
    segments = lax.axis_size("segment")
    segment_at = lax.axis_index("segment")
    seq_at = lax.axis_index("seq")
    z, x, c = seq_at // (XN * CN), (seq_at // CN) % XN, seq_at % CN
    tok_dev, width = queue.shape[1], queue.shape[2]
    up = [(i, (i + 1) % segments) for i in range(segments)]
    down = [((i + 1) % segments, i) for i in range(segments)]

    half = tok_dev // 2
    one_hot = order_matrix()
    order = jnp.asarray(one_hot, jnp.bfloat16)

    def ordered(w):
        return jnp.dot(w, order, preferred_element_type=jnp.float32).astype(jnp.bfloat16)

    def table(zz, position):
        places = [zz * XN * CN + ((x + r) % XN) * CN + c for r in (0, XN - 1, 1, 2)]
        return rope_tables(position, places, tok_dev)

    w_raw = w_qkv[0].reshape(width, 3 * HEAD)
    w_out_own = w_out[0]
    w_got = on_seq(w_raw, C_SWAP)
    normed = norm_rows(queue[0])
    z_normed, below, above = on_seq(normed, Z_SWAP), on_seq(normed, X_UP), on_seq(normed, X_DOWN)

    levels, normed = tie(levels, normed)
    picked = levels[:, None] == jnp.arange(plan.shape[0], dtype=jnp.int32)[None, :]
    step_values = jnp.sum(jnp.where(picked, plan[None, :], 0), axis=1)
    embedding = jax.nn.silu(time_embedding(step_values, width)).astype(jnp.bfloat16)
    mod = jnp.dot(embedding, w_mod[0], preferred_element_type=jnp.float32)
    mod, w_raw = tie(mod, w_raw)
    w_mine = ordered(w_raw)
    mod = gather_step(mod, C_SWAP, c)
    mod, w_mine, below, above, positions = tie(mod, w_mine, below, above, positions)
    top, low = below[:half], above[half:]
    mod = gather_step(mod, X_PAIR, x % 2)
    mod, top, low, positions = tie(mod, top, low, positions)
    far_top, far_low = on_seq(top, X_UP), on_seq(low, X_DOWN)
    near_table = table(z, positions[0])
    mod = gather_step(mod, X_FAR, x // 2)
    mod, w_got, positions, *near_table = tie(mod, w_got, positions, *near_table)
    w_other = ordered(w_got)
    mod = gather_step(mod, Z_SWAP, z)
    gains = jnp.sum(jnp.concatenate([q_gain, k_gain])[:, :, None] * jnp.asarray(one_hot[None, :HEAD, :HEAD]), axis=1)
    gq = gains[:1] * (HEAD**-0.5 * math.log2(math.e))
    gk = gains[1:]
    z_normed, far_top, far_low, w_out_own, positions, gq, gk = tie(
        z_normed, far_top, far_low, w_out_own, positions, gq, gk
    )
    z_below, z_above = on_seq(z_normed, X_UP), on_seq(z_normed, X_DOWN)
    w_far = on_seq(w_out_own, Z_SWAP)
    far_table = table(1 - z, positions[0])
    modulation = mod.reshape(1, -1)
    shift_row = modulation[:, :width]
    scale_row = 1.0 + modulation[:, width : 2 * width]
    gate_row = modulation[:, 2 * width :]

    def half_frame(limit, blocks, tables):
        return qkv(limit, blocks, scale_row, shift_row, *tables, gq, gk, w_mine, w_other)

    def with_partner(q_mine, kv_mine, other):
        got = on_seq(other, C_SWAP)
        return (q_mine, got), jnp.concatenate([kv_mine, got[:, HEAD:]], axis=0)

    def halo(kv):
        return lax.ppermute(kv, "segment", up), lax.ppermute(kv, "segment", down)

    near_half = half_frame(60 << 20, (normed, below, above, far_top, far_low), near_table)
    z_below, z_above, *near_half = tie(z_below, z_above, *near_half)
    top, low = z_below[:half], z_above[half:]
    top, low, w_out_own, *near_half = tie(top, low, w_out_own, *near_half)
    w_below, w_above = on_seq(w_out_own, X_UP), on_seq(w_out_own, X_DOWN)
    z_far_top, z_far_low = on_seq(top, X_UP), on_seq(low, X_DOWN)
    q_near, kv_near = with_partner(*near_half)
    halo_near = halo(kv_near)
    z_normed, z_far_top, kv_near, w_far = tie(z_normed, z_far_top, kv_near, w_far)
    far_half = half_frame(LIMIT, (z_normed, z_below, z_above, z_far_top, z_far_low), far_table)
    q_far, kv_far = with_partner(*far_half)
    kv_far, *halo_near = tie(kv_far, *halo_near)
    halo_far = halo(kv_far)
    flags = jnp.stack([segment_at > 0, segment_at < segments - 1]).astype(jnp.int32)
    queries = (*q_near, *q_far)
    first = attend(flags, queries, (kv_near, kv_far, *halo_near), ((None, (0, 1)), (0, (2,)), (1, (3,))))
    w_below, w_above, w_far, old_out, old_sum, *halo_far = tie(w_below, w_above, w_far, *first, *halo_far)
    top, low = w_below[:half], w_above[half:]
    near_w = [w_out_own, w_below, w_above, on_seq(top, X_UP), on_seq(low, X_DOWN)]
    w_below, w_above = on_seq(w_far, X_UP), on_seq(w_far, X_DOWN)
    near, theirs = attend(flags, queries, halo_far, ((0, (0,)), (1, (1,))), (old_out, old_sum))
    far = on_seq(theirs, Z_SWAP)
    near, w_below, w_above = tie(near, w_below, w_above)
    top, low = w_below[:half], w_above[half:]
    near, top, low = tie(near, top, low)
    far_w = [w_far, w_below, w_above, on_seq(top, X_UP), on_seq(low, X_DOWN)]
    sides = pair_heads(near, far)
    a_parts = [sides[0], on_seq(sides[2], X_UP), on_seq(sides[1], X_DOWN), on_seq(sides[3], X_FAR)]
    w_parts = []
    for at in range(4):
        for block in (near_w, far_w):
            w_parts += block[at : at + 1] if at < 3 else block[3:5]
    mine, other = out_project(a_parts, w_parts)
    side_n = 4
    last = segments - 1
    finished, *pieces = finish(side_n, queue[0], gate_row, mine, on_seq(other, C_SWAP))
    arrived = lax.ppermute(finished, "segment", up[:-1])
    queue_next = jnp.where(segment_at == 0, fresh_noise, arrived)[None]

    columns = width // segments
    spread = jnp.where(segment_at == last, pieces[-1], jnp.zeros((), jnp.bfloat16))
    for place in range(side_n - 1):
        spread += lax.ppermute(pieces[place], "segment", [(last, last - (side_n - 1) + place)])
    clean = jnp.where(segment_at >= segments - side_n, spread[:, (side_n - 1) * columns :], jnp.zeros((), jnp.bfloat16))
    for row in range(side_n - 1):
        clean += lax.ppermute(
            spread[:, row * columns : (row + 1) * columns],
            "segment",
            [(segments - side_n + place, row * side_n + place) for place in range(side_n)],
        )
    return (queue_next, clean)


def solution(mesh):
    placed = (
        P("segment", "seq", None),
        P("seq", None),
        P("segment", None, "seq"),
        P("segment", None, "seq", None),
        P("segment", "seq", None),
        P("segment", None),
        P("segment", None),
        P("segment"),
        P(),
        P("segment"),
    )
    return jax.shard_map(
        shards,
        mesh=mesh,
        in_specs=placed,
        out_specs=(P("segment", "seq", None), P("seq", "segment")),
        check_vma=False,
    )
```

```python
import functools
import math

import jax
import jax.numpy as jnp
import numpy as np
from jax import lax
from jax.experimental import pallas as pl
from jax.experimental.pallas import tpu as pltpu
from jax.sharding import PartitionSpec as P

GRID_W = 32
EPSILON = 1e-06
ROPE_BASE = 256.0
HEAD = 128
NEG = -1e30
XN, CN, ZN = 4, 2, 2
VMEM = pl.BlockSpec(memory_space=pltpu.VMEM)
SMEM = pl.BlockSpec(memory_space=pltpu.SMEM)
LIMIT = 32 << 20


def seq_id(z, x, c):
    return (z % ZN) * XN * CN + (x % XN) * CN + (c % CN)


ALL = [(z, x, c) for z in range(ZN) for x in range(XN) for c in range(CN)]
X_UP = [(seq_id(z, x, c), seq_id(z, x + 1, c)) for z, x, c in ALL]
X_DOWN = [(seq_id(z, x, c), seq_id(z, x - 1, c)) for z, x, c in ALL]
X_FAR = [(seq_id(z, x, c), seq_id(z, x + 2, c)) for z, x, c in ALL]
X_PAIR = [(seq_id(z, x, c), seq_id(z, x ^ 1, c)) for z, x, c in ALL]
Z_SWAP = [(seq_id(z, x, c), seq_id(z + 1, x, c)) for z, x, c in ALL]
C_SWAP = [(seq_id(z, x, c), seq_id(z, x, c + 1)) for z, x, c in ALL]


def on_seq(value, pairs):
    return lax.ppermute(value, "seq", pairs)


def tie(*values):
    return lax.optimization_barrier(values)


def lane_order():
    time_dim = HEAD // 8
    space_dim = (HEAD - time_dim) // 2
    first, second, start = [], [], 0
    for section in (time_dim, space_dim, space_dim):
        half = section // 2
        first += list(range(start, start + half))
        second += list(range(start + half, start + section))
        start += section
    return np.array(first + second)


ORDER = lane_order()


def order_matrix():
    one = np.zeros((3 * HEAD, 3 * HEAD), np.float32)
    for part in range(2):
        one[part * HEAD + ORDER, part * HEAD + np.arange(HEAD)] = 1.0
    one[2 * HEAD + np.arange(HEAD), 2 * HEAD + np.arange(HEAD)] = 1.0
    return one


def time_embedding(step_values, width):
    half_width = width // 2
    counter = jnp.arange(half_width, dtype=jnp.float32)
    frequency = jnp.exp(-jnp.log(10000.0) * counter / half_width)
    angles = step_values.astype(jnp.float32)[:, None] * frequency[None, :]
    return jnp.concatenate([jnp.cos(angles), jnp.sin(angles)], axis=-1)


def rope_frequencies():
    time_dim = HEAD // 8
    space_dim = (HEAD - time_dim) // 2
    lanes = np.zeros((3, HEAD), np.float32)
    start = 0
    for at, section in enumerate((time_dim, space_dim, space_dim)):
        half = section // 2
        power = np.float32(ROPE_BASE) ** (np.float32(-2.0) * np.arange(half, dtype=np.float32) / np.float32(section))
        lanes[at, start : start + half] = power
        lanes[at, HEAD // 2 + start : HEAD // 2 + start + half] = power
        start += half
    return lanes


def rope_tables(position, places, tok_dev):
    lanes = jnp.asarray(rope_frequencies())
    sign = jnp.where(jnp.arange(HEAD) < HEAD // 2, -1.0, 1.0)
    rows = tok_dev // GRID_W
    grid_row = (jnp.stack(places)[:, None] * rows + jnp.arange(rows, dtype=jnp.int32)).astype(jnp.float32)
    grid_col = jnp.arange(GRID_W, dtype=jnp.int32).astype(jnp.float32)
    by_row = position.astype(jnp.float32) * lanes[0] + grid_row[..., None] * lanes[1]
    by_col = grid_col[:, None] * lanes[2]
    column = lanes[2] > 0
    tables = []
    for turn, factor in ((jnp.cos, 1.0), (jnp.sin, sign)):
        table = jnp.where(column, (turn(by_col) * factor)[None, None], (turn(by_row) * factor)[:, :, None])
        tables.append(table.reshape(-1, HEAD))
    return tuple(tables)


def norm_kernel(x_ref, o_ref):
    x = x_ref[...].astype(jnp.float32)
    centre = jnp.mean(x, axis=-1, keepdims=True)
    x = x - centre
    spread = jnp.mean(x * x, axis=-1, keepdims=True)
    o_ref[...] = (x * lax.rsqrt(spread + EPSILON)).astype(jnp.bfloat16)


def norm_rows(x):
    rows, width = x.shape
    block = 64
    return pl.pallas_call(
        norm_kernel,
        grid=(rows // block,),
        in_specs=[pl.BlockSpec((block, width), lambda i: (i, 0))],
        out_specs=pl.BlockSpec((block, width), lambda i: (i, 0)),
        out_shape=jax.ShapeDtypeStruct(x.shape, jnp.bfloat16),
        cost_estimate=pl.CostEstimate(flops=1, bytes_accessed=1, transcendentals=0),
        name="norm_rows",
    )(x)


def qkv_kernel(count, scale_ref, shift_ref, cos_ref, sin_ref, gq_ref, gk_ref, w_mine, w_other, *refs):
    x_refs = refs[:count]
    q_mine, kv_mine, all_other, acc = refs[count:]
    step = pl.program_id(0)
    x = jnp.concatenate([r[...] for r in x_refs], axis=0).astype(jnp.float32)
    x = (x * scale_ref[...] + shift_ref[...]).astype(jnp.bfloat16)
    w = jnp.concatenate([w_mine[...], w_other[...]], axis=1)
    part = jnp.dot(x, w, preferred_element_type=jnp.float32)

    @pl.when(step == 0)
    def _():
        acc[...] = part

    @pl.when(step > 0)
    def _():
        acc[...] += part

    @pl.when(step == pl.num_programs(0) - 1)
    def _():
        cos, sin = cos_ref[...], sin_ref[...]

        def turned(y, gain):
            y = y * lax.rsqrt(jnp.mean(y * y, axis=-1, keepdims=True) + EPSILON) * gain
            return (y * cos + pltpu.roll(y, HEAD // 2, 1) * sin).astype(jnp.bfloat16)

        q_mine[...] = turned(acc[:, :HEAD], gq_ref[...])
        kv_mine[:, :HEAD] = turned(acc[:, HEAD : 2 * HEAD], gk_ref[...])
        kv_mine[:, HEAD:] = acc[:, 2 * HEAD : 3 * HEAD].astype(jnp.bfloat16)
        all_other[:, :HEAD] = turned(acc[:, 3 * HEAD : 4 * HEAD], gq_ref[...])
        all_other[:, HEAD : 2 * HEAD] = turned(acc[:, 4 * HEAD : 5 * HEAD], gk_ref[...])
        all_other[:, 2 * HEAD :] = acc[:, 5 * HEAD :].astype(jnp.bfloat16)


def qkv(limit, blocks, scale, shift, cos, sin, gq, gk, w_mine, w_other):
    width = w_mine.shape[0]
    rows = sum(b.shape[0] for b in blocks)
    depth = 1536
    row_spec = pl.BlockSpec((1, depth), lambda k: (0, k))
    whole = lambda a: pl.BlockSpec(a.shape, lambda k: (0, 0))
    w_spec = pl.BlockSpec((depth, 3 * HEAD), lambda k: (k, 0))
    out = [jax.ShapeDtypeStruct((rows, n), jnp.bfloat16) for n in (HEAD, 2 * HEAD, 3 * HEAD)]
    return pl.pallas_call(
        functools.partial(qkv_kernel, len(blocks)),
        grid=(width // depth,),
        in_specs=[row_spec, row_spec, whole(cos), whole(sin), whole(gq), whole(gk), w_spec, w_spec]
        + [pl.BlockSpec((b.shape[0], depth), lambda k: (0, k)) for b in blocks],
        out_specs=[pl.BlockSpec(o.shape, lambda k: (0, 0)) for o in out],
        out_shape=out,
        scratch_shapes=[pltpu.VMEM((rows, 6 * HEAD), jnp.float32)],
        compiler_params=pltpu.CompilerParams(vmem_limit_bytes=limit),
        cost_estimate=pl.CostEstimate(flops=1, bytes_accessed=1, transcendentals=0),
        name="qkv",
    )(scale, shift, cos, sin, gq, gk, w_mine, w_other, *blocks)


def attend_kernel(flag_ref, *refs):
    q_in, kv_in, o_refs = refs[:4], refs[4:10], refs[10:12]
    q_a, q_b, kv_all, sems = refs[12:]
    kv_refs = [kv_all.at[i] for i in range(6)]
    copies = [pltpu.make_async_copy(q_in[i], (q_a, q_b)[i % 2].at[i // 2], sems.at[6 + i]) for i in range(4)]
    copies += [pltpu.make_async_copy(kv_in[i], kv_refs[i], sems.at[i]) for i in range(6)]
    for copy in copies:
        copy.start()
    for copy in copies[:4]:
        copy.wait()
    blocks = q_a.shape[1] // HEAD
    chunk = 512
    per = kv_all.shape[1] // chunk
    state = [(None, None)] * 4
    for group in range(3):
        flag = None if group == 0 else flag_ref[group - 1] > 0
        parts = [(kv_refs[2 * group + i], j * chunk) for i in range(2) for j in range(per)]
        for copy in copies[4 + 2 * group : 6 + 2 * group]:
            copy.wait()
        for at, q_ref in enumerate((q_a.at[0], q_b.at[0], q_a.at[1], q_b.at[1])):
            q = q_ref[:, :HEAD]
            acc, m = state[at]
            scores = [
                lax.dot_general(
                    q,
                    ref[row : row + chunk, :HEAD],
                    (((1,), (1,)), ((), ())),
                    preferred_element_type=jnp.float32,
                )
                for ref, row in parts
            ]
            top = functools.reduce(jnp.maximum, [jnp.max(s, axis=1, keepdims=True) for s in scores])
            if flag is not None:
                top = jnp.where(flag, top, NEG)
            later = top if m is None else jnp.maximum(m, top)
            less = later if flag is None else jnp.where(flag, later, -NEG)
            total = None
            for score, (ref, row) in zip(scores, parts):
                p = jnp.exp2(score - less).astype(jnp.bfloat16)
                v = ref[row : row + chunk, HEAD:]
                v = jnp.concatenate([v, jnp.ones_like(v)], axis=1)
                d = jnp.dot(p, v, preferred_element_type=jnp.float32)
                total = d if total is None else total + d
            acc = total if acc is None else acc * jnp.exp2(m - later) + total
            state[at] = (acc, later)
    for at, (acc, _) in enumerate(state):
        o = (acc[:, :HEAD] / acc[:, HEAD:]).astype(jnp.bfloat16)
        for block in range(blocks):
            row = (2 * block + at % 2) * HEAD
            o_refs[at // 2][row : row + HEAD, :] = o[block * HEAD : (block + 1) * HEAD]


def attend(flags, queries, key_values):
    rows = 2 * queries[0].shape[0]
    return pl.pallas_call(
        attend_kernel,
        in_specs=[SMEM] + [pl.BlockSpec(memory_space=pl.ANY)] * (4 + len(key_values)),
        out_specs=[VMEM] * 2,
        out_shape=[jax.ShapeDtypeStruct((rows, HEAD), jnp.bfloat16)] * 2,
        scratch_shapes=[
            pltpu.VMEM((2, *queries[0].shape), jnp.bfloat16),
            pltpu.VMEM((2, *queries[1].shape), jnp.bfloat16),
            pltpu.VMEM((len(key_values), *key_values[0].shape), jnp.bfloat16),
            pltpu.SemaphoreType.DMA((4 + len(key_values),)),
        ],
        compiler_params=pltpu.CompilerParams(vmem_limit_bytes=60 << 20),
        cost_estimate=pl.CostEstimate(flops=1, bytes_accessed=1, transcendentals=0),
        name="attend",
    )(flags, *queries, *key_values)


def pair_kernel(near_ref, far_ref, *outs):
    rows = outs[0].shape[0]
    for at, out in enumerate(outs):
        out[:, :HEAD] = near_ref[at * rows : (at + 1) * rows, :]
        out[:, HEAD:] = far_ref[at * rows : (at + 1) * rows, :]


def pair_heads(near, far):
    rows = near.shape[0] // XN
    return pl.pallas_call(
        pair_kernel,
        in_specs=[VMEM] * 2,
        out_specs=[VMEM] * XN,
        out_shape=[jax.ShapeDtypeStruct((rows, 2 * HEAD), jnp.bfloat16)] * XN,
        cost_estimate=pl.CostEstimate(flops=1, bytes_accessed=1, transcendentals=0),
        name="pair_heads",
    )(near, far)


def out_kernel(count, *refs):
    a_refs = refs[:4]
    w_refs = refs[4 : 4 + count]
    mine, other = refs[4 + count :]
    a = jnp.concatenate([r[...] for r in a_refs], axis=1)
    w = jnp.concatenate([r[...] for r in w_refs], axis=0)
    part = jnp.dot(a, w, preferred_element_type=jnp.float32)
    rows = mine.shape[0]
    mine[...] = part[:rows]
    other[...] = part[rows:].astype(jnp.bfloat16)


def out_project(a_parts, w_parts):
    rows = a_parts[0].shape[0] // 2
    width = w_parts[0].shape[1]
    depth = sum(w.shape[0] for w in w_parts)
    step = 512
    return pl.pallas_call(
        functools.partial(out_kernel, len(w_parts)),
        grid=(width // step,),
        in_specs=[pl.BlockSpec(a.shape, lambda n: (0, 0)) for a in a_parts]
        + [pl.BlockSpec((w.shape[0], step), lambda n: (0, n)) for w in w_parts],
        out_specs=[pl.BlockSpec((rows, step), lambda n: (0, n))] * 2,
        out_shape=[
            jax.ShapeDtypeStruct((rows, width), jnp.float32),
            jax.ShapeDtypeStruct((rows, width), jnp.bfloat16),
        ],
        compiler_params=pltpu.CompilerParams(vmem_limit_bytes=60 << 20),
        cost_estimate=pl.CostEstimate(flops=1, bytes_accessed=1, transcendentals=0),
        name="out_project",
    )(*a_parts, *w_parts)


def gather_step(part, pairs, bit):
    got = on_seq(part, pairs)
    return jnp.concatenate([jnp.where(bit == 0, part, got), jnp.where(bit == 0, got, part)], axis=0)


def finish_kernel(side_n, queue_ref, gate_ref, mine_ref, got_ref, sent_ref, *pieces):
    width = queue_ref.shape[1]
    columns = width // (side_n * side_n)
    projected = mine_ref[...] + got_ref[...].astype(jnp.float32)
    finished = (queue_ref[...].astype(jnp.float32) + gate_ref[...] * projected).astype(jnp.bfloat16)
    for place, piece in enumerate(pieces):
        for row in range(side_n):
            at = (row * side_n + place) * columns
            piece[:, row * columns : (row + 1) * columns] = finished[:, at : at + columns]
    sent_ref[...] = finished


def finish(side_n, queue, gate, mine, got):
    rows, width = queue.shape
    step = 32
    spec = lambda n: pl.BlockSpec((step, n), lambda i: (i, 0))
    out = [jax.ShapeDtypeStruct((rows, width), jnp.bfloat16)]
    out += [jax.ShapeDtypeStruct((rows, width // side_n), jnp.bfloat16)] * side_n
    return pl.pallas_call(
        functools.partial(finish_kernel, side_n),
        grid=(rows // step,),
        in_specs=[spec(width), pl.BlockSpec((1, width), lambda i: (0, 0)), spec(width), spec(width)],
        out_specs=[spec(o.shape[1]) for o in out],
        out_shape=out,
        compiler_params=pltpu.CompilerParams(vmem_limit_bytes=60 << 20),
        cost_estimate=pl.CostEstimate(flops=1, bytes_accessed=1, transcendentals=0),
        name="finish",
    )(queue, gate, mine, got)


def shards(queue, fresh_noise, w_mod, w_qkv, w_out, q_gain, k_gain, levels, plan, positions):
    segments = lax.axis_size("segment")
    segment_at = lax.axis_index("segment")
    seq_at = lax.axis_index("seq")
    z, x, c = seq_at // (XN * CN), (seq_at // CN) % XN, seq_at % CN
    tok_dev, width = queue.shape[1], queue.shape[2]
    up = [(i, (i + 1) % segments) for i in range(segments)]
    down = [((i + 1) % segments, i) for i in range(segments)]

    half = tok_dev // 2
    one_hot = order_matrix()
    order = jnp.asarray(one_hot, jnp.bfloat16)

    def ordered(w):
        return jnp.dot(w, order, preferred_element_type=jnp.float32).astype(jnp.bfloat16)

    def table(zz, position):
        places = [zz * XN * CN + ((x + r) % XN) * CN + c for r in (0, XN - 1, 1, 2)]
        return rope_tables(position, places, tok_dev)

    w_raw = w_qkv[0].reshape(width, 3 * HEAD)
    w_out_own = w_out[0]
    w_got = on_seq(w_raw, C_SWAP)
    normed = norm_rows(queue[0])
    z_normed, below, above = on_seq(normed, Z_SWAP), on_seq(normed, X_UP), on_seq(normed, X_DOWN)

    levels, normed = tie(levels, normed)
    picked = levels[:, None] == jnp.arange(plan.shape[0], dtype=jnp.int32)[None, :]
    step_values = jnp.sum(jnp.where(picked, plan[None, :], 0), axis=1)
    embedding = jax.nn.silu(time_embedding(step_values, width)).astype(jnp.bfloat16)
    mod = jnp.dot(embedding, w_mod[0], preferred_element_type=jnp.float32)
    mod, w_raw = tie(mod, w_raw)
    w_mine = ordered(w_raw)
    mod = gather_step(mod, C_SWAP, c)
    mod, w_mine, below, above, positions = tie(mod, w_mine, below, above, positions)
    top, low = below[:half], above[half:]
    mod = gather_step(mod, X_PAIR, x % 2)
    mod, top, low, positions = tie(mod, top, low, positions)
    far_top, far_low = on_seq(top, X_UP), on_seq(low, X_DOWN)
    near_table = table(z, positions[0])
    mod = gather_step(mod, X_FAR, x // 2)
    mod, w_got, positions, *near_table = tie(mod, w_got, positions, *near_table)
    w_other = ordered(w_got)
    mod = gather_step(mod, Z_SWAP, z)
    gains = jnp.sum(jnp.concatenate([q_gain, k_gain])[:, :, None] * jnp.asarray(one_hot[None, :HEAD, :HEAD]), axis=1)
    gq = gains[:1] * (HEAD**-0.5 * math.log2(math.e))
    gk = gains[1:]
    z_normed, far_top, far_low, w_out_own, positions, gq, gk = tie(
        z_normed, far_top, far_low, w_out_own, positions, gq, gk
    )
    z_below, z_above = on_seq(z_normed, X_UP), on_seq(z_normed, X_DOWN)
    w_far = on_seq(w_out_own, Z_SWAP)
    far_table = table(1 - z, positions[0])
    modulation = mod.reshape(1, -1)
    shift_row = modulation[:, :width]
    scale_row = 1.0 + modulation[:, width : 2 * width]
    gate_row = modulation[:, 2 * width :]

    def half_frame(limit, blocks, tables):
        return qkv(limit, blocks, scale_row, shift_row, *tables, gq, gk, w_mine, w_other)

    def with_partner(q_mine, kv_mine, other):
        got = on_seq(other, C_SWAP)
        return (q_mine, got), jnp.concatenate([kv_mine, got[:, HEAD:]], axis=0)

    def halo(kv):
        return lax.ppermute(kv, "segment", up), lax.ppermute(kv, "segment", down)

    near_half = half_frame(60 << 20, (normed, below, above, far_top, far_low), near_table)
    z_below, z_above, *near_half = tie(z_below, z_above, *near_half)
    top, low = z_below[:half], z_above[half:]
    top, low, w_out_own, *near_half = tie(top, low, w_out_own, *near_half)
    w_below, w_above = on_seq(w_out_own, X_UP), on_seq(w_out_own, X_DOWN)
    z_far_top, z_far_low = on_seq(top, X_UP), on_seq(low, X_DOWN)
    q_near, kv_near = with_partner(*near_half)
    halo_near = halo(kv_near)
    z_normed, z_far_top, kv_near, w_far = tie(z_normed, z_far_top, kv_near, w_far)
    far_half = half_frame(LIMIT, (z_normed, z_below, z_above, z_far_top, z_far_low), far_table)
    q_far, kv_far = with_partner(*far_half)
    kv_far, w_below, w_above = tie(kv_far, w_below, w_above)
    halo_far = halo(kv_far)
    top, low = w_below[:half], w_above[half:]
    top, low, w_far, *halo_far = tie(top, low, w_far, *halo_far)
    near_w = [w_out_own, w_below, w_above, on_seq(top, X_UP), on_seq(low, X_DOWN)]

    flags = jnp.stack([segment_at > 0, segment_at < segments - 1]).astype(jnp.int32)
    w_below, w_above = on_seq(w_far, X_UP), on_seq(w_far, X_DOWN)
    key_values = (kv_near, kv_far, halo_near[0], halo_far[0], halo_near[1], halo_far[1])
    near, theirs = attend(flags, (*q_near, *q_far), key_values)
    far = on_seq(theirs, Z_SWAP)
    near, w_below, w_above = tie(near, w_below, w_above)
    top, low = w_below[:half], w_above[half:]
    near, top, low = tie(near, top, low)
    far_w = [w_far, w_below, w_above, on_seq(top, X_UP), on_seq(low, X_DOWN)]
    sides = pair_heads(near, far)
    a_parts = [sides[0], on_seq(sides[2], X_UP), on_seq(sides[1], X_DOWN), on_seq(sides[3], X_FAR)]
    w_parts = []
    for at in range(4):
        for block in (near_w, far_w):
            w_parts += block[at : at + 1] if at < 3 else block[3:5]
    mine, other = out_project(a_parts, w_parts)
    side_n = 4
    last = segments - 1
    finished, *pieces = finish(side_n, queue[0], gate_row, mine, on_seq(other, C_SWAP))
    arrived = lax.ppermute(finished, "segment", up[:-1])
    queue_next = jnp.where(segment_at == 0, fresh_noise, arrived)[None]

    columns = width // segments
    spread = jnp.where(segment_at == last, pieces[-1], jnp.zeros((), jnp.bfloat16))
    for place in range(side_n - 1):
        spread += lax.ppermute(pieces[place], "segment", [(last, last - (side_n - 1) + place)])
    clean = jnp.where(segment_at >= segments - side_n, spread[:, (side_n - 1) * columns :], jnp.zeros((), jnp.bfloat16))
    for row in range(side_n - 1):
        clean += lax.ppermute(
            spread[:, row * columns : (row + 1) * columns],
            "segment",
            [(segments - side_n + place, row * side_n + place) for place in range(side_n)],
        )
    return (queue_next, clean)


def solution(mesh):
    placed = (
        P("segment", "seq", None),
        P("seq", None),
        P("segment", None, "seq"),
        P("segment", None, "seq", None),
        P("segment", "seq", None),
        P("segment", None),
        P("segment", None),
        P("segment"),
        P(),
        P("segment"),
    )
    return jax.shard_map(
        shards,
        mesh=mesh,
        in_specs=placed,
        out_specs=(P("segment", "seq", None), P("seq", "segment")),
        check_vma=False,
    )
```
